32 devices in a mesh: groups: 1, ado: 8 (over z, y), row: 2 (over x), sub: 2 (over core).
Axes of the slice: x: 2, y: 2, z: 4, core: 2. Of those that a mesh axis runs over, the one named last changes fastest.
Arguments:
- state: bfloat16 [768, 2, 128, 128], P(('groups', 'ado', 'sub'), None, 'row'), may hold values from -6 to 6
- hamiltonian: bfloat16 [2, 128, 128], P('groups'), may hold values from -0.5 to 0.5
- coupling: float32 [96, 128], replicated, may hold values from -3 to 3
- damping: float32 [96], replicated, may hold values from 0.05 to 1
- coef_re: float32 [96], replicated, may hold values from 0.2 to 2
- coef_im: float32 [96], replicated, may hold values from -3 to 3
- link_owner: int32 [768, 6], P(('groups', 'ado', 'sub')), may hold values from 0 to 15, all different within a row; in each aligned block of 48 rows (0 to 47, 48 to 95, ...) at most 27 rows name the same one
- link_slot: int32 [768, 6], P(('groups', 'ado', 'sub')), may hold values from 0 to 47
- link_mode: int32 [768, 6], P(('groups', 'ado', 'sub')), may hold values from 0 to 95
- link_weight: int32 [768, 6], P(('groups', 'ado', 'sub')), may hold values from 0 to 4
Outputs:
- derivative: bfloat16 [768, 2, 128, 128], P(('groups', 'ado', 'sub'), None, 'row')
The draws below stay inside these ranges and needn't reach their ends.
Inputs may be any that keep to these rules, and one draw needn't show every extreme that they name: `link_owner`: among the links of the operators of one device (aligned blocks of 48 operators), no value is named by more than 27 links, and in every draw some value is named by exactly 27; the links of one operator name different values.
All inputs are finite; a program needn't handle non-finite values.
Results may differ from the reference program's by a relative error of at most 0.001.
Values may be sent and summed in bfloat16 or wider, within the bound.
A program may use at most 128 MiB of HBM per device.

```python
import math
import jax
import jax.numpy as jnp
import numpy as np
from jax import lax

S = 128
K = 96
UP = 4
ADO_DEV = 48
LINKS = 6
ADOS = 768
CAP = 27
N_ADO = 8
N_SUB = 2


def place_ends(entries, key, least, top_value):
    spot = [jax.random.randint(jax.random.fold_in(key, axis), (), 0, length) for axis, length in enumerate(entries.shape)]
    main_axis = entries.shape.index(max(entries.shape))
    beside = spot[:main_axis] + [(spot[main_axis] + 1) % entries.shape[main_axis]] + spot[main_axis + 1:]
    return entries.at[tuple(spot)].set(least).at[tuple(beside)].set(top_value)


def block_scale(rng, shape, shards, low, largest):
    factor_of, own = 1.0, jax.random.fold_in(rng, 6)
    for position, parts in shards:
        steps = jnp.exp(jax.random.uniform(jax.random.fold_in(own, position), (parts,), jnp.float32, low / len(shards), largest / len(shards)))
        factor_of = factor_of * jnp.repeat(steps, shape[position] // parts).reshape([-1 if axis == position else 1 for axis in range(len(shape))])
    return factor_of


def deal_out(stream_key, own, number, rows, number_of, top, most, slope):
    ranking = jax.random.permutation(stream_key, number_of)
    heavy_load, common = portions_of(number_of, rows * top, most, slope, True), portions_of(number_of, rows * top, most, slope, False)
    places = jnp.arange(number_of)

    def named(sizes, rotation):
        used = int((sizes > 0).sum())
        fixed = max(1, used // 4)
        passed = fixed + (places - fixed + rotation * (used - fixed)) % max(1, number_of - fixed)
        return jnp.zeros((number_of,), jnp.int32).at[ranking[jnp.where(places < fixed, places, passed)]].set(jnp.asarray(sizes, jnp.int32))

    sizes = jnp.where(number % 4 == 0, named(heavy_load, number // 4), named(common, number - number // 4 - 1))
    mixed = jax.random.permutation(jax.random.fold_in(own, 3), number_of)
    source_of, sink = mixed[0:number_of // 2 * 2:2], mixed[1:number_of // 2 * 2:2]
    margin = jnp.minimum(sizes[source_of] - 1, most - sizes[sink]) // 2
    margin = jnp.where((source_of == ranking[0]) | (sink == ranking[0]) | (sizes[sink] == 0), 0, jnp.maximum(margin, 0))
    passed = jax.random.randint(jax.random.fold_in(own, 4), (number_of // 2,), 0, 1 << 20) % (margin + 1)
    sizes = sizes.at[source_of].add(-passed).at[sink].add(passed)
    items = jnp.searchsorted(jnp.cumsum(sizes), jnp.arange(rows * top), side="right").astype(jnp.int32)
    grid = items.reshape(top, rows).T
    grid = grid[jax.random.permutation(jax.random.fold_in(own, 1), rows)]
    rotation = jax.random.randint(jax.random.fold_in(own, 2), (rows, 1), 0, top)
    return jnp.take_along_axis(grid, (jnp.arange(top)[None, :] + rotation) % top, axis=1)


def portions_of(amount, total, most, slope, full):
    loads = [(1 << 20) // math.isqrt(rank ** slope) + 1 for rank in range(1, amount + 1)]
    largest = most if full else min(most, max(-(-total // amount), total * loads[0] // sum(loads)))
    least = 1 if total - largest >= amount - 1 else 0
    given, surplus = [largest] + [least] * (amount - 1), total - largest - least * (amount - 1)
    while surplus > 0:
        movable = [i for i in range(1, amount) if given[i] < largest] or [i for i in range(1, amount) if given[i] < most]
        whole, left = sum([loads[i] for i in movable]), surplus
        for i in movable:
            addition = min(most - given[i], max(1, left * loads[i] // whole), surplus)
            given[i] = given[i] + addition
            surplus = surplus - addition
    return np.array(given)


def centred(key, shape, spread, bound, shards=(), kind=jnp.bfloat16):
    loudness = block_scale(key, shape, shards, -0.22, 0.18) if shards else 1.0
    values = jax.random.normal(key, shape, jnp.float32) * spread * loudness
    return jnp.minimum(jnp.maximum(values, -bound), bound).astype(kind)


def setup_inputs(seed: int = 0, part: int = 0) -> dict:
    streams_of = jax.random.split(jax.random.key(seed), 11)
    part_splits = jax.random.split(jax.random.fold_in(streams_of[10], part), 11)
    state = centred(part_splits[0], (ADOS, 2, S, S), 1.0, 6.0, ((0, 16), (2, 2)))
    hamiltonian = centred(part_splits[1], (2, S, S), S ** -0.5, 0.5)
    coupling = centred(streams_of[2], (K, S), 0.5, 3.0, (), jnp.float32)
    damping = jnp.clip(jnp.exp(jax.random.uniform(streams_of[3], (K,), jnp.float32, math.log(0.05), math.log(1.0))), 0.05, 1.0)
    coef_re = jnp.clip(jnp.exp(jax.random.uniform(streams_of[4], (K,), jnp.float32, math.log(0.2), math.log(2.0))), 0.2, 2.0)
    coef_im = centred(streams_of[5], (K,), 0.5, 3.0, (), jnp.float32)
    link_owner_keys = jax.random.split(jax.random.fold_in(part_splits[6], 1), ADOS // ADO_DEV)
    link_owner_turns = jax.random.permutation(jax.random.fold_in(part_splits[6], 3), ADOS // ADO_DEV)
    link_owner = jax.vmap(lambda own, number: deal_out(jax.random.fold_in(part_splits[6], 2), own, number, ADO_DEV, N_ADO * N_SUB, LINKS, CAP, 2))(link_owner_keys, link_owner_turns).reshape((ADOS, LINKS))
    link_slot = place_ends(jax.random.randint(part_splits[7], (ADOS, LINKS), 0, ADO_DEV), jax.random.fold_in(part_splits[7], 1), 0, ADO_DEV - 1).astype(jnp.int32)
    link_mode = place_ends(jax.random.randint(part_splits[8], (ADOS, LINKS), 0, K), jax.random.fold_in(part_splits[8], 1), 0, K - 1).astype(jnp.int32)
    link_weight = place_ends(jax.random.randint(part_splits[9], (ADOS, LINKS), 0, 5), jax.random.fold_in(part_splits[9], 1), 0, 4).astype(jnp.int32)
    return {"state": state, "hamiltonian": hamiltonian, "coupling": coupling, "damping": damping, "coef_re": coef_re, "coef_im": coef_im, "link_owner": link_owner, "link_slot": link_slot, "link_mode": link_mode, "link_weight": link_weight}


def link_terms(rho_rows, neighbours, link_mode, link_weight, coupling, coupling_rows, damping, coef_re, coef_im):
    modes_all = coupling.shape[0]
    select = (link_mode[:, :, None] == jnp.arange(modes_all)[None, None, :]).astype(jnp.float32)
    scale = jnp.sqrt(jnp.sqrt(coef_re * coef_re + coef_im * coef_im))
    params = jnp.stack([coef_re, coef_im, scale, damping], 1)
    picked = jnp.einsum('alk,kp->alp', select, params, precision=lax.Precision.HIGHEST)
    mode_re = picked[:, :, 0]
    mode_im = picked[:, :, 1]
    mode_scale = picked[:, :, 2]
    mode_damp = picked[:, :, 3]
    upward = (jnp.arange(link_mode.shape[1]) < UP)[None, :]
    weight_f = link_weight.astype(jnp.float32)
    root = jnp.sqrt(weight_f)
    turn = jnp.where(upward, root * mode_scale, root * mode_re / mode_scale)
    plus = jnp.where(upward, jnp.float32(0.0), root * mode_im / mode_scale)
    decay = lax.optimization_barrier(jnp.sum(jnp.where(upward, jnp.float32(0.0), weight_f * mode_damp), 1))
    vec_rows = jnp.einsum('alk,kr->alr', select, coupling_rows, precision=lax.Precision.HIGHEST)
    vec_cols = jnp.einsum('alk,ks->als', select, coupling, precision=lax.Precision.HIGHEST)
    gap = vec_rows[:, :, :, None] - vec_cols[:, :, None, :]
    total = vec_rows[:, :, :, None] + vec_cols[:, :, None, :]
    near_re = neighbours[:, :, 0].astype(jnp.float32)
    near_im = neighbours[:, :, 1].astype(jnp.float32)
    first = turn[:, :, None, None] * gap
    second = plus[:, :, None, None] * total
    link_re = lax.optimization_barrier(jnp.sum(first * near_im + second * near_re, 1))
    link_im = lax.optimization_barrier(jnp.sum(second * near_im - first * near_re, 1))
    rho_re = rho_rows[:, 0].astype(jnp.float32)
    rho_im = rho_rows[:, 1].astype(jnp.float32)
    return (link_re - decay[:, None, None] * rho_re, link_im - decay[:, None, None] * rho_im)

def right_product(rho_rows, hamiltonian):

    def product(left, right):
        return jnp.einsum('ars,st->art', left.astype(jnp.float32), right.astype(jnp.float32), precision=lax.Precision.HIGHEST)
    rho_re = rho_rows[:, 0]
    rho_im = rho_rows[:, 1]
    return (product(rho_re, hamiltonian[0]) - product(rho_im, hamiltonian[1]), product(rho_re, hamiltonian[1]) + product(rho_im, hamiltonian[0]))

def reference(state, hamiltonian, coupling, damping, coef_re, coef_im, link_owner, link_slot, link_mode, link_weight):
    ados = state.shape[0]
    blocks = ados // ADO_DEV
    index = (link_owner * ADO_DEV + link_slot).astype(jnp.int32)

    def left_product(left, right):
        return jnp.einsum('rc,acs->ars', left.astype(jnp.float32), right.astype(jnp.float32), precision=lax.Precision.HIGHEST)

    def one_block(block):
        start = (block * ADO_DEV).astype(jnp.int32)
        rho_rows = lax.dynamic_slice_in_dim(state, start, ADO_DEV, 0)
        block_index = lax.dynamic_slice_in_dim(index, start, ADO_DEV, 0)
        block_mode = lax.dynamic_slice_in_dim(link_mode, start, ADO_DEV, 0)
        block_weight = lax.dynamic_slice_in_dim(link_weight, start, ADO_DEV, 0)
        neighbours = jnp.take(state, block_index.reshape(-1), axis=0).reshape(block_index.shape + state.shape[1:])
        left_re = left_product(hamiltonian[0], rho_rows[:, 0]) - left_product(hamiltonian[1], rho_rows[:, 1])
        left_im = left_product(hamiltonian[0], rho_rows[:, 1]) + left_product(hamiltonian[1], rho_rows[:, 0])
        right_re, right_im = right_product(rho_rows, hamiltonian)
        link_re, link_im = link_terms(rho_rows, neighbours, block_mode, block_weight, coupling, coupling, damping, coef_re, coef_im)
        out_re = left_im - right_im + link_re
        out_im = right_re - left_re + link_im
        return jnp.stack([out_re, out_im], 1).astype(jnp.bfloat16)
    result = lax.map(one_block, jnp.arange(blocks, dtype=jnp.int32))
    return result.reshape(state.shape)
```

```python
import jax
import jax.numpy as jnp
from jax import lax
from jax.experimental import pallas as pl
from jax.experimental.pallas import tpu as pltpu
from jax.sharding import PartitionSpec as P

UP = 4


def link_terms(
    rho_rows, neighbours, link_mode, link_weight, coupling, coupling_rows, damping, coef_re, coef_im
):
    modes_all = coupling.shape[0]
    select = (link_mode[:, :, None] == jnp.arange(modes_all)[None, None, :]).astype(jnp.float32)
    scale = jnp.sqrt(jnp.sqrt(coef_re * coef_re + coef_im * coef_im))
    params = jnp.stack([coef_re, coef_im, scale, damping], 1)
    picked = jnp.einsum("alk,kp->alp", select, params, precision=lax.Precision.HIGHEST)
    mode_re = picked[:, :, 0]
    mode_im = picked[:, :, 1]
    mode_scale = picked[:, :, 2]
    mode_damp = picked[:, :, 3]
    upward = (jnp.arange(link_mode.shape[1]) < UP)[None, :]
    weight_f = link_weight.astype(jnp.float32)
    root = jnp.sqrt(weight_f)
    turn = jnp.where(upward, root * mode_scale, root * mode_re / mode_scale)
    plus = jnp.where(upward, jnp.float32(0.0), root * mode_im / mode_scale)
    decay = jnp.sum(jnp.where(upward, jnp.float32(0.0), weight_f * mode_damp), 1)
    vec_rows = jnp.einsum("alk,kr->alr", select, coupling_rows, precision=lax.Precision.HIGHEST)
    vec_cols = jnp.einsum("alk,ks->als", select, coupling, precision=lax.Precision.HIGHEST)
    gap = vec_rows[:, :, :, None] - vec_cols[:, :, None, :]
    total = vec_rows[:, :, :, None] + vec_cols[:, :, None, :]
    near_re = neighbours[:, :, 0].astype(jnp.float32)
    near_im = neighbours[:, :, 1].astype(jnp.float32)
    first = turn[:, :, None, None] * gap
    second = plus[:, :, None, None] * total
    link_re = jnp.sum(first * near_im + second * near_re, 1)
    link_im = jnp.sum(second * near_im - first * near_re, 1)
    rho_re = rho_rows[:, 0].astype(jnp.float32)
    rho_im = rho_rows[:, 1].astype(jnp.float32)
    return (link_re - decay[:, None, None] * rho_re, link_im - decay[:, None, None] * rho_im)


def product_left(left, right):
    return jnp.einsum("rc,acs->ars", left, right, preferred_element_type=jnp.float32)


def product_right(left, right):
    return jnp.einsum("ars,st->art", left, right, preferred_element_type=jnp.float32)


def body(
    state,
    hamiltonian,
    coupling,
    damping,
    coef_re,
    coef_im,
    link_owner,
    link_slot,
    link_mode,
    link_weight,
):
    ados, _, rows, sites = state.shape
    links = link_owner.shape[1]
    peers = lax.axis_size(("ado", "sub"))
    capacity = max(2, min(ados, 3 * ados * links // (2 * peers)))
    row_start = lax.axis_index("row") * rows
    ham_rows = lax.dynamic_slice_in_dim(hamiltonian, row_start, rows, 1)
    coupling_rows = lax.dynamic_slice_in_dim(coupling, row_start, rows, 1)
    piece = lax.all_gather(state, "row", axis=2, tiled=True)
    part_re = product_left(ham_rows[0], piece[:, 0]) - product_left(ham_rows[1], piece[:, 1])
    part_im = product_left(ham_rows[0], piece[:, 1]) + product_left(ham_rows[1], piece[:, 0])
    owner_flat = link_owner.reshape(-1)
    slot_flat = link_slot.reshape(-1)
    onehot = (owner_flat[:, None] == jnp.arange(peers, dtype=jnp.int32)[None, :]).astype(jnp.int32)
    rank_flat = jnp.sum((jnp.cumsum(onehot, 0) - 1) * onehot, 1)
    outgoing = jnp.zeros((peers, capacity), jnp.int32).at[owner_flat, rank_flat].set(slot_flat)
    wanted = lax.all_to_all(outgoing, ("ado", "sub"), split_axis=0, concat_axis=0, tiled=True)
    sending = jnp.take(state, wanted.reshape(-1), axis=0).reshape(peers, capacity, 2, rows, sites)
    arrived = lax.all_to_all(sending, ("ado", "sub"), split_axis=0, concat_axis=0, tiled=True)
    arrived = arrived.reshape(peers * capacity, 2, rows, sites)
    neighbours = jnp.take(arrived, owner_flat * capacity + rank_flat, axis=0).reshape(
        ados, links, 2, rows, sites
    )
    right_re = product_right(state[:, 0], hamiltonian[0]) - product_right(
        state[:, 1], hamiltonian[1]
    )
    right_im = product_right(state[:, 0], hamiltonian[1]) + product_right(
        state[:, 1], hamiltonian[0]
    )
    link_re, link_im = link_terms(
        state,
        neighbours,
        link_mode,
        link_weight,
        coupling,
        coupling_rows,
        damping,
        coef_re,
        coef_im,
    )
    out_re = part_im - right_im + link_re
    out_im = right_re - part_re + link_im
    return jnp.stack([out_re, out_im], 1).astype(jnp.bfloat16)


MESH = pl.DeviceIdType.MESH
CHUNKS = 4
IN, OUT, SIDE, PAIR = 0, 1, 2, 3

END_IN = [
    (1, 0, 0, (SIDE,)),
    (1, 0, 1, ()),
    (2, 0, 0, (SIDE,)),
    (2, 0, 1, (SIDE,)),
    (3, 0, 0, (SIDE,)),
    (3, 0, 1, (SIDE,)),
    (1, 1, 1, ()),
]
END_SIDE = [
    (0, 1, 0, (IN,)),
    (0, 1, 1, (IN,)),
    (1, 1, 0, ()),
    (2, 1, 0, ()),
    (2, 1, 1, ()),
    (3, 1, 0, ()),
    (3, 1, 1, ()),
]
MID_IN = [
    (2, 0, 0, (OUT, SIDE)),
    (2, 0, 1, (OUT, SIDE)),
    (3, 0, 0, (OUT,)),
    (3, 0, 1, (OUT,)),
    (3, 1, 0, ()),
    (3, 1, 1, ()),
]
MID_OUT = [(0, 0, 0, (IN,)), (0, 0, 1, (IN,)), (0, 1, 0, (IN,)), (0, 1, 1, (IN,))]
MID_SIDE = [(1, 1, 0, ()), (1, 1, 1, ()), (2, 1, 0, ()), (2, 1, 1, ())]
MID_LATE = (1, 1, 1, (OUT,))


def root_of(w):
    low = jnp.where(w == 1, jnp.float32(1.0), jnp.float32(0.0))
    low = jnp.where(w == 2, jnp.float32(2.0**0.5), low)
    low = jnp.where(w == 3, jnp.float32(3.0**0.5), low)
    return jnp.where(w == 4, jnp.float32(2.0), low)


def kernel(
    state,
    ham,
    coupling,
    damping,
    coef_re,
    coef_im,
    owner,
    slot,
    mode,
    weight,
    out,
    held,
    full,
    acc,
    up_turn,
    down_turn,
    down_plus,
    right_mat,
    left_mat,
    send,
    recv,
    local,
):
    ados, _, rows, sites = state.shape
    links = owner.shape[1]
    modes = coupling.shape[0]
    a, c, r = lax.axis_index("ado"), lax.axis_index("sub"), lax.axis_index("row")
    z, y = a // 2, a % 2
    low = z < 2
    inward = jnp.where(low, 1, -1)
    place = jnp.where(low, z, 3 - z)
    at_end, at_mid = place == 0, place == 1
    to = {
        IN: {"ado": (z + inward) * 2 + y},
        OUT: {"ado": (z - inward) * 2 + y},
        SIDE: {"ado": z * 2 + 1 - y},
        PAIR: {"sub": 1 - c},
    }
    size = ados // CHUNKS
    half_chunks = CHUNKS // 2

    def ado_of(p, other):
        return jnp.where(low, p, 3 - p) * 2 + (1 - y if other else y)

    def copy(way, index, chunk, own=False):
        piece = pl.ds(chunk * size, size)
        block = index * 2 + c
        return pltpu.make_async_remote_copy(
            src_ref=state.at[piece] if own else held.at[block, piece],
            dst_ref=held.at[block, piece],
            send_sem=send.at[way, index, chunk],
            recv_sem=recv.at[block, chunk],
            device_id=to[way],
            device_id_type=MESH,
        )

    def from_pair(index, chunk):
        piece = pl.ds(chunk * size, size)
        block = index * 2 + 1 - c
        return pltpu.make_async_remote_copy(
            src_ref=held.at[block, piece],
            dst_ref=held.at[block, piece],
            send_sem=send.at[PAIR, index, chunk],
            recv_sem=recv.at[block, chunk],
            device_id=to[PAIR],
            device_id_type=MESH,
        )

    mine = pl.ds(pl.multiple_of(r * rows, rows), rows)
    row_copy = pltpu.make_async_remote_copy(
        src_ref=state,
        dst_ref=full.at[:, :, mine],
        send_sem=local.at[0],
        recv_sem=local.at[1],
        device_id={"row": 1 - r},
        device_id_type=MESH,
    )
    own_held = pltpu.make_async_copy(state, held.at[a * 2 + c], local.at[2])
    own_full = pltpu.make_async_copy(state, full.at[:, :, mine], local.at[3])

    barrier = pltpu.get_barrier_semaphore()
    for target in (to[IN], to[SIDE], to[PAIR], {"row": 1 - r}):
        pl.semaphore_signal(barrier, inc=1, device_id=target, device_id_type=MESH)

    @pl.when(at_mid)
    def _():
        pl.semaphore_signal(barrier, inc=1, device_id=to[OUT], device_id_type=MESH)
        pl.semaphore_wait(barrier, 5)

    @pl.when(at_end)
    def _():
        pl.semaphore_wait(barrier, 4)

    def own_sends(ways, act):
        for k in range(CHUNKS):
            for way in ways:
                act(copy(way, a, k, own=True))

    start = lambda d: d.start()
    done = lambda d: d.wait_send()

    own_sends((IN, SIDE), start)

    @pl.when(at_mid)
    def _():
        own_sends((OUT,), start)

    row_copy.start()
    own_held.start()
    own_full.start()
    own_sends((PAIR,), start)

    right_mat[:sites, :sites] = -ham[1]
    right_mat[:sites, sites:] = ham[0]
    right_mat[sites:, :sites] = -ham[0]
    right_mat[sites:, sites:] = -ham[1]
    left_mat[:rows, :sites] = ham[1, mine, :]
    left_mat[:rows, sites:] = ham[0, mine, :]
    left_mat[rows:, :sites] = -ham[0, mine, :]
    left_mat[rows:, sites:] = ham[1, mine, :]

    def table(k, carry):
        cols = coupling[pl.ds(k, 1), :]
        turned = jnp.transpose(jnp.broadcast_to(cols, (sites, sites)))
        here = jnp.where(r == 0, turned[:rows], turned[rows:])
        re = jnp.full((8, sites), coef_re[k])
        im = jnp.full((8, sites), coef_im[k])
        scale = jnp.sqrt(jnp.sqrt(re * re + im * im))
        gap = (here - cols).reshape(rows // 8, 8, sites)
        total = (here + cols).reshape(rows // 8, 8, sites)
        up_turn[k] = (scale * gap).reshape(rows, sites)
        down_turn[k] = (re / scale * gap).reshape(rows, sites)
        down_plus[k] = (im / scale * total).reshape(rows, sites)
        return carry

    lax.fori_loop(0, modes, table, 0)

    def product(n, carry):
        both = jnp.concatenate([full[n, 0], full[n, 1]], axis=0)
        left = jnp.dot(left_mat[...], both, preferred_element_type=jnp.float32)
        own_re, own_im = full[n, 0, mine, :], full[n, 1, mine, :]
        right = jnp.dot(
            jnp.concatenate([own_re, own_im], axis=1),
            right_mat[...],
            preferred_element_type=jnp.float32,
        )
        decay = jnp.float32(0.0)
        for j in range(UP, links):
            decay = decay + weight[n, j].astype(jnp.float32) * damping[mode[n, j]]
        acc[n, 0] = left[:rows] + right[:, :sites] - decay * own_re.astype(jnp.float32)
        acc[n, 1] = left[rows:] + right[:, sites:] - decay * own_im.astype(jnp.float32)
        return carry

    def products(part):
        third = ados // 3
        if part == 0:
            row_copy.wait_recv()
            own_full.wait()
        lax.fori_loop(part * third, (part + 1) * third, product, 0)

    def chunks_of(half):
        return range(half * half_chunks, (half + 1) * half_chunks)

    def run(streams, late):
        for s in range(max(len(stream) for stream in streams)):
            for i in range(half_chunks):
                for stream in streams:
                    if s < len(stream):
                        p, other, half, ways = stream[s]
                        index, k = ado_of(p, other), half * half_chunks + i
                        copy(PAIR, index, k).wait_recv()
                        for way in ways + (PAIR,):
                            copy(way, index, k).start()
            if s == 4 and late is not None:
                for k in chunks_of(late[2]):
                    for way in late[3]:
                        copy(way, ado_of(late[0], late[1]), k).start()
            if 2 <= s <= 4:
                products(s - 2)

    def drain(streams, late):
        for stream in list(streams) + ([[late]] if late is not None else []):
            for p, other, half, ways in stream:
                for k in chunks_of(half):
                    for way in ways + (() if stream == [late] else (PAIR,)):
                        copy(way, ado_of(p, other), k).wait_send()

    @pl.when(at_end)
    def _():
        run((END_IN, END_SIDE), None)

    @pl.when(at_mid)
    def _():
        run((MID_IN, MID_OUT, MID_SIDE), MID_LATE)

    own_held.wait()
    for index in range(8):
        for k in range(CHUNKS):
            from_pair(index, k).wait_recv()

    def gather(n, carry):
        sum_re, sum_im = acc[n, 0], acc[n, 1]
        for j in range(links):
            o, s, k = owner[n, j], slot[n, j], mode[n, j]
            root = root_of(weight[n, j])
            near = held[o, s].astype(jnp.float32)
            near_re, near_im = near[0], near[1]
            first = root * (up_turn[k] if j < UP else down_turn[k])
            sum_re = sum_re + first * near_im
            sum_im = sum_im - first * near_re
            if j >= UP:
                second = root * down_plus[k]
                sum_re = sum_re + second * near_re
                sum_im = sum_im + second * near_im
        out[n, 0] = sum_re.astype(jnp.bfloat16)
        out[n, 1] = sum_im.astype(jnp.bfloat16)
        return carry

    lax.fori_loop(0, ados, gather, 0)

    own_sends((IN, SIDE, PAIR), done)
    row_copy.wait_send()

    @pl.when(at_mid)
    def _():
        own_sends((OUT,), done)
        drain((MID_IN, MID_OUT, MID_SIDE), MID_LATE)

    @pl.when(at_end)
    def _():
        drain((END_IN, END_SIDE), None)


def fused(*args):
    state, coupling = args[0], args[2]
    ados, _, rows, sites = state.shape
    modes = coupling.shape[0]
    peers = lax.axis_size(("ado", "sub"))
    chips = peers // 2
    vmem = pl.BlockSpec(memory_space=pltpu.VMEM)
    smem = pl.BlockSpec(memory_space=pltpu.SMEM)
    return pl.pallas_call(
        kernel,
        out_shape=jax.ShapeDtypeStruct(state.shape, jnp.bfloat16),
        in_specs=[pl.BlockSpec(memory_space=pl.ANY), vmem, vmem] + [smem] * 7,
        out_specs=vmem,
        scratch_shapes=[
            pltpu.VMEM((peers, ados, 2, rows, sites), jnp.bfloat16),
            pltpu.VMEM((ados, 2, 2 * rows, sites), jnp.bfloat16),
            pltpu.VMEM((ados, 2, rows, sites), jnp.float32),
            pltpu.VMEM((modes, rows, sites), jnp.float32),
            pltpu.VMEM((modes, rows, sites), jnp.float32),
            pltpu.VMEM((modes, rows, sites), jnp.float32),
            pltpu.VMEM((2 * sites, 2 * sites), jnp.bfloat16),
            pltpu.VMEM((2 * rows, 2 * sites), jnp.bfloat16),
            pltpu.SemaphoreType.DMA((4, chips, CHUNKS)),
            pltpu.SemaphoreType.DMA((peers, CHUNKS)),
            pltpu.SemaphoreType.DMA((4,)),
        ],
        compiler_params=pltpu.CompilerParams(
            collective_id=0, has_side_effects=True, vmem_limit_bytes=56 * 1024 * 1024
        ),
    )(*args)


def solution(mesh):
    grid = mesh.shape["groups"] == 1 and mesh.shape["ado"] == 8
    grid = grid and mesh.shape["row"] == 2 and mesh.shape["sub"] == 2
    step = fused if grid else body
    placed = (
        P(("groups", "ado", "sub"), None, "row", None),
        P("groups", None, None),
        P(),
        P(),
        P(),
        P(),
        P(("groups", "ado", "sub"), None),
        P(("groups", "ado", "sub"), None),
        P(("groups", "ado", "sub"), None),
        P(("groups", "ado", "sub"), None),
    )
    return jax.shard_map(
        step,
        mesh=mesh,
        in_specs=placed,
        out_specs=P(("groups", "ado", "sub"), None, "row", None),
        check_vma=False,
    )
```
